32 devices in a mesh: space: 8 (over z, x), chan: 4 (over y, core).
Axes of the slice: x: 2, y: 2, z: 4, core: 2. Of those that a mesh axis runs over, the one named last changes fastest.
Arguments:
- inputs: bfloat16 [16, 256, 1024], P(None, 'chan', 'space'), may hold values from -6 to 6
- kernel_one: bfloat16 [256, 3, 3, 256], P('chan'), may hold values from -0.125 to 0.125
- kernel_two: bfloat16 [256, 3, 3, 256], P('chan'), may hold values from -0.125 to 0.125
- cotangent: bfloat16 [16, 256, 1024], P(None, 'chan', 'space'), may hold values from -6 to 6
Outputs:
- result: bfloat16 [16, 256, 1024], P(None, 'chan', 'space')
- grad_inputs: bfloat16 [16, 256, 1024], P(None, 'chan', 'space')
- grad_kernel_one: float32 [256, 3, 3, 256], P('chan')
- grad_kernel_two: float32 [256, 3, 3, 256], P('chan')
The draws below stay inside these ranges and needn't reach their ends.
All inputs are finite; a program needn't handle non-finite values.
Results may differ from the reference program's by a relative error of at most 0.019.
Values may be sent and summed in bfloat16 or wider, within the bound.
A program may use at most 64 MiB of HBM per device.

```python
import jax
import jax.numpy as jnp
from jax import lax

C = 256
ROWS = 16
COLS = 1024


def block_scale(rng, extent, cuts, smallest, largest):
    def one(position, blocks):
        heights = jax.random.uniform(jax.random.fold_in(jax.random.fold_in(rng, 6), position), (blocks,), jnp.float32, smallest / len(cuts), largest / len(cuts))
        return jnp.repeat(jnp.exp(heights), extent[position] // blocks).reshape((-1,) + (1,) * (len(extent) - position - 1))

    loudness = one(*cuts[0])
    for cut in cuts[1:]:
        loudness = loudness * one(*cut)
    return loudness


def normal_values(key, shape, deviation, most, cuts=(), held_as=jnp.bfloat16):
    drawn = deviation * jax.random.normal(key, shape, jnp.float32)
    if cuts:
        drawn = drawn * block_scale(key, shape, cuts, -0.22, 0.18)
    return jnp.clip(drawn, -most, most).astype(held_as)


def setup_inputs(seed: int = 0) -> dict:
    arg_keys = jax.random.split(jax.random.key(seed), 5)
    return {
        "inputs": normal_values(arg_keys[0], (ROWS, C, COLS), 1.0, 6.0, ((1, 4), (2, 8))),
        "kernel_one": normal_values(arg_keys[1], (C, 3, 3, C), (9 * C) ** -0.5, 0.125, ((0, 4),)),
        "kernel_two": normal_values(arg_keys[2], (C, 3, 3, C), (9 * C) ** -0.5, 0.125, ((0, 4),)),
        "cotangent": normal_values(arg_keys[3], (ROWS, C, COLS), 1.0, 6.0, ((1, 4), (2, 8))),
    }


def convolve(values, kernel):
    return lax.conv_general_dilated(values[None], kernel, (1, 1), ((1, 1), (1, 1)), dimension_numbers=("NHCW", "OHWI", "NHCW"), preferred_element_type=jnp.float32)[0]


def flipped(kernel):
    return jnp.transpose(kernel[:, ::-1, ::-1], (3, 1, 2, 0))


def silu_slope(preact):
    sigmoid_part = jax.nn.sigmoid(preact)
    return sigmoid_part * (1.0 + preact * (1.0 - sigmoid_part))


def tap_products(values, gradient):
    padded = jnp.pad(values, ((1, 1), (0, 0), (1, 1))).astype(jnp.float32)
    height, width = gradient.shape[0], gradient.shape[2]
    grad_wide = gradient.astype(jnp.float32)
    pieces = []
    for row_tap in range(3):
        for col_tap in range(3):
            window = padded[row_tap:row_tap + height, :, col_tap:col_tap + width]
            pieces.append(jnp.einsum("hiw,how->oi", window, grad_wide))
    return jnp.stack(pieces, axis=1).reshape(gradient.shape[1], 3, 3, values.shape[1])


def reference(inputs, kernel_one, kernel_two, cotangent):
    pre_one = convolve(inputs, kernel_one)
    hidden = jax.nn.silu(pre_one).astype(jnp.bfloat16)
    pre_two = convolve(hidden, kernel_two)
    result = jax.nn.silu(pre_two).astype(jnp.bfloat16)
    grad_two = (cotangent.astype(jnp.float32) * silu_slope(pre_two)).astype(jnp.bfloat16)
    grad_kernel_two = tap_products(hidden, grad_two)
    grad_hidden = convolve(grad_two, flipped(kernel_two))
    grad_one = (grad_hidden * silu_slope(pre_one)).astype(jnp.bfloat16)
    grad_kernel_one = tap_products(inputs, grad_one)
    grad_inputs = convolve(grad_one, flipped(kernel_one)).astype(jnp.bfloat16)
    return result, grad_inputs, grad_kernel_one, grad_kernel_two
```

```python
import functools

import jax
import jax.numpy as jnp
from jax import lax
from jax.experimental import pallas as pl
from jax.experimental.pallas import tpu as pltpu
from jax.sharding import PartitionSpec as P

F32 = jnp.float32
BF16 = jnp.bfloat16
MESH = pl.DeviceIdType.MESH
LANES = 128
CHUNKS = 4


def kernel(
    n, reduce_here, x_ref, k1_ref, k2_ref, cot_ref, result_ref, gin_ref, g1_ref, g2_ref,
    blocks, halo_in, halo_out, cat_one, cat_two, cat_back, weight, partial, slope_one,
    grad_rows, kt_out, kt_in, sum_out, sum_in, sum_all,
    st_send, st_recv, halo_send, halo_recv, kt_send, kt_recv, rs_send, rs_recv, ag_send, ag_recv,
):
    s, c = lax.axis_index("space"), lax.axis_index("chan")
    rows, chans = x_ref.shape[0], x_ref.shape[1]
    full = 4 * chans
    wide = 3 * full
    left, right = lax.rem(s + n - 1, n), lax.rem(s + 1, n)
    sibling = c + 1 - 2 * lax.rem(c, 2)
    across = lax.rem(c + 2, 4)
    lane = lax.broadcasted_iota(jnp.int32, (chans, LANES), 1)
    lane_full = lax.broadcasted_iota(jnp.int32, (full, LANES), 1)

    def remote(src, dst, send, recv, to_s, to_c):
        return pltpu.make_async_remote_copy(
            src_ref=src, dst_ref=dst, send_sem=send, recv_sem=recv,
            device_id={"space": to_s, "chan": to_c}, device_id_type=MESH,
        )

    barrier = pltpu.get_barrier_semaphore()
    count = 0
    for d in range(1, 4):
        pl.semaphore_signal(barrier, inc=1, device_id={"space": s, "chan": lax.rem(c + d, 4)}, device_id_type=MESH)
        count += 1
    for side in (left, right):
        for j in range(4):
            pl.semaphore_signal(barrier, inc=1, device_id={"space": side, "chan": j}, device_id_type=MESH)
            count += 1
    if reduce_here:
        for d in range(2, n - 1):
            pl.semaphore_signal(barrier, inc=1, device_id={"space": lax.rem(s + d, n), "chan": c}, device_id_type=MESH)
            count += 1

    def edge_step(p, value, low, high):
        low = jnp.where(lane == p, pltpu.roll(value, p, 1), low)
        high = jnp.where(lane == p, pltpu.roll(value, lax.rem(p + 1, LANES), 1), high)
        return low, high

    zero_edge = jnp.zeros((chans, LANES), F32)
    pending = []

    def send_stage(t, low, high):
        halo_out[t, 0] = low.astype(BF16)
        halo_out[t, 1] = high.astype(BF16)
        started = []
        for j in range(4):
            for side, to in ((0, left), (1, right)):
                copy = remote(
                    halo_out.at[t, side], halo_in.at[t, 1 - side, c],
                    halo_send.at[t, side, j], halo_recv.at[t, 1 - side, c], to, j,
                )
                copy.start()
                pending.append(copy)
        step = rows // CHUNKS
        across_copies, near_copies = [], []
        for k in range(CHUNKS):
            part = pl.ds(k * step, step)
            copy = remote(
                blocks.at[t, c, part], blocks.at[t, c, part],
                st_send.at[t, 0, k], st_recv.at[t, 0, k], s, across,
            )
            copy.start()
            pending.append(copy)
            across_copies.append(copy)
        for k in range(CHUNKS):
            part = pl.ds(k * step, step)
            copy = remote(
                blocks.at[t, c, part], blocks.at[t, c, part],
                st_send.at[t, 1, k], st_recv.at[t, 1, k], s, sibling,
            )
            copy.start()
            pending.append(copy)
            near_copies.append(copy)
        return across_copies, near_copies

    def forward_stage(t, copies):
        across_copies, near_copies = copies
        step = rows // CHUNKS
        forwards = []
        for k in range(CHUNKS):
            across_copies[k].wait_recv()
            part = pl.ds(k * step, step)
            copy = remote(
                blocks.at[t, across, part], blocks.at[t, across, part],
                st_send.at[t, 2, k], st_recv.at[t, 2, k], s, sibling,
            )
            copy.start()
            pending.append(copy)
            forwards.append(copy)
        return forwards + near_copies

    def collect_stage(t, waits, cat):
        for j in range(4):
            for side in range(2):
                remote(
                    halo_out.at[t, side], halo_in.at[t, side, j],
                    halo_send.at[t, side, j], halo_recv.at[t, side, j], left, j,
                ).wait_recv()
        for copy in waits:
            copy.wait_recv()
        from_left = halo_in[t, 0].reshape(full, LANES).astype(F32)
        from_right = halo_in[t, 1].reshape(full, LANES).astype(F32)
        from_left = jnp.where(s > 0, from_left, 0.0)
        from_right = jnp.where(s < n - 1, from_right, 0.0)
        cat[:, 0:LANES] = jnp.zeros((wide, LANES), BF16)
        cat[:, (rows + 1) * LANES:] = jnp.zeros((wide, LANES), BF16)

        def body(p, _):
            value = blocks[t, :, p].reshape(full, LANES)
            value32 = value.astype(F32)
            at = pl.ds(pl.multiple_of((p + 1) * LANES, LANES), LANES)
            low = jnp.where(
                lane_full == 0, pltpu.roll(from_left, lax.rem(LANES - p, LANES), 1), pltpu.roll(value32, 1, 1)
            )
            high = jnp.where(
                lane_full == LANES - 1, pltpu.roll(from_right, LANES - 1 - p, 1), pltpu.roll(value32, LANES - 1, 1)
            )
            cat[0:full, at] = low.astype(BF16)
            cat[full:2 * full, at] = value
            cat[2 * full:, at] = high.astype(BF16)
            return 0

        lax.fori_loop(0, rows, body, 0)

    def conv(cat):
        def body(t, _):
            at = pl.ds(pl.multiple_of(t * 2 * LANES, 2 * LANES), 2 * LANES)
            partial[:, at] = jnp.dot(weight[...], cat[:, at], preferred_element_type=F32)
            return 0

        lax.fori_loop(0, (rows + 2) // 2, body, 0)

    def preact(p):
        total = None
        for a in range(3):
            at = pl.ds(pl.multiple_of((p + a) * LANES, LANES), LANES)
            term = partial[a * chans:(a + 1) * chans, at]
            total = term if total is None else total + term
        return total

    def set_weight(k_ref):
        for a in range(3):
            weight[a * chans:(a + 1) * chans, :] = k_ref[:, a * wide:(a + 1) * wide]

    def put_grad(p, value):
        for a in range(3):
            at = pl.ds(pl.multiple_of((p + a) * LANES, LANES), LANES)
            grad_rows[a * chans:(a + 1) * chans, at] = value

    def sum_piece(k):
        return (
            pl.ds(pl.multiple_of((k // 2) * 16, 16), 16),
            pl.ds(pl.multiple_of(lax.rem(k, 2) * (3 * wide // 2), LANES), 3 * wide // 2),
        )

    def kernel_gradient(layer, cat, out_ref):
        total = lax.dot_general(
            grad_rows[...], cat[...], (((1,), (1,)), ((), ())), preferred_element_type=F32
        )
        if not reduce_here:
            for a in range(3):
                out_ref[:, a * wide:(a + 1) * wide] = total[a * chans:(a + 1) * chans]
            return []
        for a in range(3):
            sum_out[layer, :, a * wide:(a + 1) * wide] = total[a * chans:(a + 1) * chans].astype(BF16)
        copies = []
        for d in range(1, n):
            to = lax.rem(s + d, n)
            rr, ll = sum_piece(to)
            copy = remote(
                sum_out.at[layer, rr, ll], sum_in.at[layer, d],
                rs_send.at[layer, d], rs_recv.at[layer, d], to, c,
            )
            copy.start()
            pending.append(copy)
            copies.append(copy)
        return copies

    def kernel_sum(layer, copies):
        rr, ll = sum_piece(s)
        total = sum_out[layer, rr, ll].astype(F32)
        for d in range(1, n):
            copies[d - 1].wait_recv()
            total = total + sum_in[layer, d].astype(F32)
        sum_all[layer, rr, ll] = total.astype(BF16)
        out = []
        for d in range(1, n):
            to = lax.rem(s + d, n)
            copy = remote(
                sum_all.at[layer, rr, ll], sum_all.at[layer, rr, ll],
                ag_send.at[layer, d], ag_recv.at[layer, d], to, c,
            )
            copy.start()
            pending.append(copy)
            out.append(copy)
        return out

    def send_taps(layer):
        copies = []
        for d in range(1, 4):
            copy = remote(
                kt_out.at[layer, lax.rem(c + d, 4)], kt_in.at[layer, c],
                kt_send.at[layer, d], kt_recv.at[layer, d], s, lax.rem(c + d, 4),
            )
            copy.start()
            pending.append(copy)
            copies.append(copy)
        return copies

    def set_back_weight(layer, copies):
        for copy in copies:
            copy.wait_recv()
        taps = kt_in[layer].reshape(full, kt_in.shape[3]).astype(F32).T.astype(BF16)
        for a in range(3):
            for b in range(3):
                tap = (2 - a) * 3 + 2 - b
                weight[a * chans:(a + 1) * chans, b * full:(b + 1) * full] = taps[tap * chans:(tap + 1) * chans]

    def first(p, edges):
        value = x_ref[p]
        blocks[0, c, p] = value
        return edge_step(p, value.astype(F32), *edges)

    low, high = lax.fori_loop(0, rows, first, (zero_edge, zero_edge))
    pl.semaphore_wait(barrier, count)
    copies = send_stage(0, low, high)
    for layer, k_ref in ((0, k1_ref), (1, k2_ref)):
        for j in range(4):
            for tap in range(9):
                kt_out[layer, j, :, tap * chans:(tap + 1) * chans] = (
                    k_ref[:, tap * full + j * chans:tap * full + (j + 1) * chans]
                )
            kt_out[layer, j, :, 9 * chans:] = jnp.zeros((chans, kt_out.shape[3] - 9 * chans), BF16)
        kt_in[layer, c] = kt_out[layer, c]
    back_two = send_taps(1)
    set_weight(k1_ref)
    grad_rows[...] = jnp.zeros(grad_rows.shape, BF16)
    collect_stage(0, forward_stage(0, copies), cat_one)
    conv(cat_one)

    def second(p, edges):
        pre = preact(p)
        sig = jax.nn.sigmoid(pre)
        slope_one[p] = sig * (1.0 + pre * (1.0 - sig))
        value = (pre * sig).astype(BF16)
        blocks[1, c, p] = value
        return edge_step(p, value.astype(F32), *edges)

    low, high = lax.fori_loop(0, rows, second, (zero_edge, zero_edge))

    copies = send_stage(1, low, high)
    back_one = send_taps(0)
    set_weight(k2_ref)
    collect_stage(1, forward_stage(1, copies), cat_two)
    conv(cat_two)

    def third(p, edges):
        pre = preact(p)
        sig = jax.nn.sigmoid(pre)
        result_ref[p] = (pre * sig).astype(BF16)
        value = (cot_ref[p].astype(F32) * (sig * (1.0 + pre * (1.0 - sig)))).astype(BF16)
        blocks[2, c, p] = value
        put_grad(p, value)
        return edge_step(p, value.astype(F32), *edges)

    low, high = lax.fori_loop(0, rows, third, (zero_edge, zero_edge))

    copies = send_stage(2, low, high)
    set_back_weight(1, back_two)
    reduce_two = kernel_gradient(1, cat_two, g2_ref)
    collect_stage(2, forward_stage(2, copies), cat_back)
    conv(cat_back)

    def fourth(p, edges):
        value = (preact(p) * slope_one[p]).astype(BF16)
        blocks[3, c, p] = value
        put_grad(p, value)
        return edge_step(p, value.astype(F32), *edges)

    low, high = lax.fori_loop(0, rows, fourth, (zero_edge, zero_edge))

    copies = send_stage(3, low, high)
    reduce_one = kernel_gradient(0, cat_one, g1_ref)
    set_back_weight(0, back_one)
    waits = forward_stage(3, copies)
    gather_two = kernel_sum(1, reduce_two) if reduce_here else []
    gather_one = kernel_sum(0, reduce_one) if reduce_here else []
    collect_stage(3, waits, cat_back)
    conv(cat_back)

    def last(p, _):
        gin_ref[p] = preact(p).astype(BF16)
        return 0

    lax.fori_loop(0, rows, last, 0)

    if reduce_here:
        for layer, out, ref in ((1, gather_two, g2_ref), (0, gather_one, g1_ref)):
            for copy in out:
                copy.wait_recv()
            ref[...] = sum_all[layer].astype(F32)
    for copy in pending:
        copy.wait_send()


def local(n, inputs, kernel_one, kernel_two, cotangent):
    rows, chans, cols = inputs.shape
    full = 4 * chans
    wide = 3 * full
    reduce_here = n == 8
    lanes = (rows + 2) * LANES
    taps = -(-9 * chans // LANES) * LANES
    dma = pltpu.SemaphoreType.DMA
    vmem = pl.BlockSpec(memory_space=pltpu.VMEM)
    result, grad_inputs, sum_one, sum_two = pl.pallas_call(
        functools.partial(kernel, n, reduce_here),
        out_shape=(
            jax.ShapeDtypeStruct((rows, chans, cols), BF16),
            jax.ShapeDtypeStruct((rows, chans, cols), BF16),
            jax.ShapeDtypeStruct((chans, 3 * wide), F32),
            jax.ShapeDtypeStruct((chans, 3 * wide), F32),
        ),
        in_specs=[vmem] * 4,
        out_specs=[vmem] * 4,
        scratch_shapes=[
            pltpu.VMEM((4, 4, rows, chans, LANES), BF16),
            pltpu.VMEM((4, 2, 4, chans, LANES), BF16),
            pltpu.VMEM((4, 2, chans, LANES), BF16),
            pltpu.VMEM((wide, lanes), BF16),
            pltpu.VMEM((wide, lanes), BF16),
            pltpu.VMEM((wide, lanes), BF16),
            pltpu.VMEM((3 * chans, wide), BF16),
            pltpu.VMEM((3 * chans, lanes), F32),
            pltpu.VMEM((rows, chans, LANES), F32),
            pltpu.VMEM((3 * chans, lanes), BF16),
            pltpu.VMEM((2, 4, chans, taps), BF16),
            pltpu.VMEM((2, 4, chans, taps), BF16),
            pltpu.VMEM((2, chans, 3 * wide), BF16),
            pltpu.VMEM((2, 8, 16, 3 * wide // 2), BF16),
            pltpu.VMEM((2, chans, 3 * wide), BF16),
            dma((4, 3, CHUNKS)),
            dma((4, 3, CHUNKS)),
            dma((4, 2, 4)),
            dma((4, 2, 4)),
            dma((2, 4)),
            dma((2, 4)),
            dma((2, 8)),
            dma((2, 8)),
            dma((2, 8)),
            dma((2, 8)),
        ],
        compiler_params=pltpu.CompilerParams(
            collective_id=0, has_side_effects=True, vmem_limit_bytes=48 * 1024 * 1024
        ),
    )(
        inputs,
        kernel_one.reshape(chans, 3 * wide),
        kernel_two.reshape(chans, 3 * wide),
        cotangent,
    )
    sum_one = sum_one.reshape(chans, 3, 3, full)
    sum_two = sum_two.reshape(chans, 3, 3, full)
    if not reduce_here:
        sum_one, sum_two = lax.psum((sum_one, sum_two), "space")
    return result, grad_inputs, sum_one, sum_two


def solution(mesh):
    act = P(None, "chan", "space")
    ker = P("chan", None, None, None)
    return jax.shard_map(
        functools.partial(local, mesh.shape["space"]), mesh=mesh,
        in_specs=(act, ker, ker, act), out_specs=(act, act, ker, ker), check_vma=False,
    )
```

```python
import functools

import jax
import jax.numpy as jnp
from jax import lax
from jax.experimental import pallas as pl
from jax.experimental.pallas import tpu as pltpu
from jax.sharding import PartitionSpec as P

F32 = jnp.float32
BF16 = jnp.bfloat16
MESH = pl.DeviceIdType.MESH
LANES = 128
CHUNKS = 4


def kernel(
    n, reduce_here, x_ref, k1_ref, k2_ref, cot_ref, result_ref, gin_ref, g1_ref, g2_ref,
    blocks, halo_in, halo_out, cat_one, cat_two, cat_back, weight, partial, slope_one,
    edges, grad_rows, kt_out, kt_in, sum_out, sum_in, sum_all,
    st_send, st_recv, halo_send, halo_recv, kt_send, kt_recv, rs_send, rs_recv, ag_send, ag_recv,
):
    s, c = lax.axis_index("space"), lax.axis_index("chan")
    rows, chans = x_ref.shape[0], x_ref.shape[1]
    full = 4 * chans
    wide = 3 * full
    high_piece = 9 * chans // 4
    left, right = lax.rem(s + n - 1, n), lax.rem(s + 1, n)
    sibling = c + 1 - 2 * lax.rem(c, 2)
    across = lax.rem(c + 2, 4)
    lane = lax.broadcasted_iota(jnp.int32, (chans, LANES), 1)
    lane_full = lax.broadcasted_iota(jnp.int32, (full, LANES), 1)

    def remote(src, dst, send, recv, to_s, to_c):
        return pltpu.make_async_remote_copy(
            src_ref=src, dst_ref=dst, send_sem=send, recv_sem=recv,
            device_id={"space": to_s, "chan": to_c}, device_id_type=MESH,
        )

    barrier = pltpu.get_barrier_semaphore()
    count = 0
    for d in range(1, 4):
        pl.semaphore_signal(barrier, inc=1, device_id={"space": s, "chan": lax.rem(c + d, 4)}, device_id_type=MESH)
        count += 1
    for side in (left, right):
        for j in range(4):
            pl.semaphore_signal(barrier, inc=1, device_id={"space": side, "chan": j}, device_id_type=MESH)
            count += 1
    if reduce_here:
        for d in range(2, n - 1):
            pl.semaphore_signal(barrier, inc=1, device_id={"space": lax.rem(s + d, n), "chan": c}, device_id_type=MESH)
            count += 1

    def edge_step(p, value, low, high):
        low = jnp.where(lane == p, pltpu.roll(value, p, 1), low)
        high = jnp.where(lane == p, pltpu.roll(value, lax.rem(p + 1, LANES), 1), high)
        return low, high

    zero_edge = jnp.zeros((chans, LANES), F32)
    pending = []

    def send_stage(t, low, high):
        halo_out[t, 0] = low.astype(BF16)
        halo_out[t, 1] = high.astype(BF16)
        started = []
        for j in range(4):
            for side, to in ((0, left), (1, right)):
                copy = remote(
                    halo_out.at[t, side], halo_in.at[t, 1 - side, c],
                    halo_send.at[t, side, j], halo_recv.at[t, 1 - side, c], to, j,
                )
                copy.start()
                pending.append(copy)
        step = rows // CHUNKS
        across_copies, near_copies = [], []
        for k in range(CHUNKS):
            part = pl.ds(k * step, step)
            copy = remote(
                blocks.at[t, c, part], blocks.at[t, c, part],
                st_send.at[t, 0, k], st_recv.at[t, 0, k], s, across,
            )
            copy.start()
            pending.append(copy)
            across_copies.append(copy)
        for k in range(CHUNKS):
            part = pl.ds(k * step, step)
            copy = remote(
                blocks.at[t, c, part], blocks.at[t, c, part],
                st_send.at[t, 1, k], st_recv.at[t, 1, k], s, sibling,
            )
            copy.start()
            pending.append(copy)
            near_copies.append(copy)
        return across_copies, near_copies

    def collect_stage(t, copies, cat, hook=None):
        across_copies, near_copies = copies
        step = rows // CHUNKS
        cat[:, 0:LANES] = jnp.zeros((wide, LANES), BF16)
        cat[:, (rows + 1) * LANES:] = jnp.zeros((wide, LANES), BF16)
        partial[:, 0:LANES] = jnp.zeros((3 * chans, LANES), F32)
        partial[:, (rows + 1) * LANES:] = jnp.zeros((3 * chans, LANES), F32)

        def row_step(p, _):
            value = blocks[t, :, p].reshape(full, LANES)
            at = pl.ds(pl.multiple_of((p + 1) * LANES, LANES), LANES)
            edge_low = pltpu.roll(edges[0], lax.rem(LANES - p, LANES), 1)
            edge_high = pltpu.roll(edges[1], LANES - 1 - p, 1)
            cat[0:full, at] = jnp.where(lane_full == 0, edge_low, pltpu.roll(value, 1, 1))
            cat[full:2 * full, at] = value
            cat[2 * full:, at] = jnp.where(lane_full == LANES - 1, edge_high, pltpu.roll(value, LANES - 1, 1))
            return 0

        def work(k):
            near_copies[k].wait_recv()
            forwards[k].wait_recv()
            lax.fori_loop(k * step, (k + 1) * step, row_step, 0, unroll=True)
            at = slice((k * step + 1) * LANES, ((k + 1) * step + 1) * LANES)
            partial[:, at] = jnp.dot(weight[...], cat[:, at], preferred_element_type=F32)

        forwards = []
        for k in range(CHUNKS):
            across_copies[k].wait_recv()
            part = pl.ds(k * step, step)
            copy = remote(
                blocks.at[t, across, part], blocks.at[t, across, part],
                st_send.at[t, 2, k], st_recv.at[t, 2, k], s, sibling,
            )
            copy.start()
            pending.append(copy)
            forwards.append(copy)
            if k == 0:
                for j in range(4):
                    for side in range(2):
                        remote(
                            halo_out.at[t, side], halo_in.at[t, side, j],
                            halo_send.at[t, side, j], halo_recv.at[t, side, j], left, j,
                        ).wait_recv()
                from_left = halo_in[t, 0].reshape(full, LANES).astype(F32)
                from_right = halo_in[t, 1].reshape(full, LANES).astype(F32)
                edges[0] = jnp.where(s > 0, from_left, 0.0).astype(BF16)
                edges[1] = jnp.where(s < n - 1, from_right, 0.0).astype(BF16)
            else:
                work(k - 1)
        gathered = hook() if hook is not None else []
        work(CHUNKS - 1)
        return gathered

    def preact(p):
        total = None
        for a in range(3):
            at = pl.ds(pl.multiple_of((p + a) * LANES, LANES), LANES)
            term = partial[a * chans:(a + 1) * chans, at]
            total = term if total is None else total + term
        return total

    def set_weight(k_ref):
        for a in range(3):
            for b in range(3):
                weight[a * chans:(a + 1) * chans, b * full:(b + 1) * full] = k_ref[3 * a + b]

    def put_grad(p, value):
        for a in range(3):
            at = pl.ds(pl.multiple_of((p + a) * LANES, LANES), LANES)
            grad_rows[a * chans:(a + 1) * chans, at] = value

    def sum_piece(k):
        return (
            pl.ds(pl.multiple_of((k // 2) * high_piece, 16), high_piece),
            pl.ds(pl.multiple_of(lax.rem(k, 2) * LANES, LANES), LANES),
        )

    def kernel_gradient(layer, cat, out_ref):
        total = lax.dot_general(
            grad_rows[...], cat[...], (((1,), (1,)), ((), ())), preferred_element_type=F32
        )
        for a in range(3):
            for b in range(3):
                tap = 3 * a + b
                term = total[a * chans:(a + 1) * chans, b * full:(b + 1) * full]
                if reduce_here:
                    sum_out[layer, tap * chans:(tap + 1) * chans, :] = term.astype(BF16)
                else:
                    out_ref[tap * chans:(tap + 1) * chans, :] = term
        if not reduce_here:
            return []
        copies = []
        for d in range(1, n):
            to = lax.rem(s + d, n)
            rr, ll = sum_piece(to)
            copy = remote(
                sum_out.at[layer, rr, ll], sum_in.at[layer, d],
                rs_send.at[layer, d], rs_recv.at[layer, d], to, c,
            )
            copy.start()
            pending.append(copy)
            copies.append(copy)
        return copies

    def kernel_sum(layer, copies):
        rr, ll = sum_piece(s)
        total = sum_out[layer, rr, ll].astype(F32)
        for d in range(1, n):
            copies[d - 1].wait_recv()
            total = total + sum_in[layer, d].astype(F32)
        sum_all[layer, rr, ll] = total.astype(BF16)
        out = []
        for d in range(1, n):
            to = lax.rem(s + d, n)
            copy = remote(
                sum_all.at[layer, rr, ll], sum_all.at[layer, rr, ll],
                ag_send.at[layer, d], ag_recv.at[layer, d], to, c,
            )
            copy.start()
            pending.append(copy)
            out.append(copy)
        return out

    def send_taps(layer):
        copies = []
        for d in range(1, 4):
            copy = remote(
                kt_out.at[layer, lax.rem(c + d, 4)], kt_in.at[layer, c],
                kt_send.at[layer, d], kt_recv.at[layer, d], s, lax.rem(c + d, 4),
            )
            copy.start()
            pending.append(copy)
            copies.append(copy)
        return copies

    def set_back_weight(layer, copies):
        for copy in copies:
            copy.wait_recv()
        taps = kt_in[layer].reshape(full, kt_in.shape[3]).astype(F32).T.astype(BF16)
        for a in range(3):
            for b in range(3):
                tap = (2 - a) * 3 + 2 - b
                weight[a * chans:(a + 1) * chans, b * full:(b + 1) * full] = taps[tap * chans:(tap + 1) * chans]

    def first(p, edges):
        value = x_ref[p]
        blocks[0, c, p] = value
        return edge_step(p, value.astype(F32), *edges)

    low, high = lax.fori_loop(0, rows, first, (zero_edge, zero_edge), unroll=4)
    pl.semaphore_wait(barrier, count)
    copies = send_stage(0, low, high)
    for layer, k_ref in ((0, k1_ref), (1, k2_ref)):
        for j in range(4):
            for tap in range(9):
                kt_out[layer, j, :, tap * chans:(tap + 1) * chans] = (
                    k_ref[tap, :, j * chans:(j + 1) * chans]
                )
            kt_out[layer, j, :, 9 * chans:] = jnp.zeros((chans, kt_out.shape[3] - 9 * chans), BF16)
        kt_in[layer, c] = kt_out[layer, c]
    back_two = send_taps(1)
    set_weight(k1_ref)
    grad_rows[...] = jnp.zeros(grad_rows.shape, BF16)
    collect_stage(0, copies, cat_one)

    def second(p, edges):
        pre = preact(p)
        sig = jax.nn.sigmoid(pre)
        slope_one[p] = sig * (1.0 + pre * (1.0 - sig))
        value = (pre * sig).astype(BF16)
        blocks[1, c, p] = value
        return edge_step(p, value.astype(F32), *edges)

    low, high = lax.fori_loop(0, rows, second, (zero_edge, zero_edge), unroll=4)

    copies = send_stage(1, low, high)
    back_one = send_taps(0)
    set_weight(k2_ref)
    collect_stage(1, copies, cat_two)

    def third(p, edges):
        pre = preact(p)
        sig = jax.nn.sigmoid(pre)
        result_ref[p] = (pre * sig).astype(BF16)
        value = (cot_ref[p].astype(F32) * (sig * (1.0 + pre * (1.0 - sig)))).astype(BF16)
        blocks[2, c, p] = value
        put_grad(p, value)
        return edge_step(p, value.astype(F32), *edges)

    low, high = lax.fori_loop(0, rows, third, (zero_edge, zero_edge), unroll=4)

    copies = send_stage(2, low, high)
    set_back_weight(1, back_two)
    reduce_two = kernel_gradient(1, cat_two, g2_ref)
    gather_two = collect_stage(
        2, copies, cat_back, functools.partial(kernel_sum, 1, reduce_two) if reduce_here else None
    )

    def fourth(p, edges):
        value = (preact(p) * slope_one[p]).astype(BF16)
        blocks[3, c, p] = value
        put_grad(p, value)
        return edge_step(p, value.astype(F32), *edges)

    low, high = lax.fori_loop(0, rows, fourth, (zero_edge, zero_edge), unroll=4)

    copies = send_stage(3, low, high)
    reduce_one = kernel_gradient(0, cat_one, g1_ref)
    set_back_weight(0, back_one)
    gather_one = collect_stage(
        3, copies, cat_back, functools.partial(kernel_sum, 0, reduce_one) if reduce_here else None
    )

    def last(p, _):
        gin_ref[p] = preact(p).astype(BF16)
        return 0

    lax.fori_loop(0, rows, last, 0)

    if reduce_here:
        for layer, out, ref in ((1, gather_two, g2_ref), (0, gather_one, g1_ref)):
            for copy in out:
                copy.wait_recv()
            ref[...] = sum_all[layer].astype(F32)
    for copy in pending:
        copy.wait_send()


def local(n, inputs, kernel_one, kernel_two, cotangent):
    rows, chans, cols = inputs.shape
    full = 4 * chans
    wide = 3 * full
    reduce_here = n == 8
    lanes = (rows + 2) * LANES
    taps = -(-9 * chans // LANES) * LANES
    dma = pltpu.SemaphoreType.DMA
    vmem = pl.BlockSpec(memory_space=pltpu.VMEM)
    result, grad_inputs, sum_one, sum_two = pl.pallas_call(
        functools.partial(kernel, n, reduce_here),
        out_shape=(
            jax.ShapeDtypeStruct((rows, chans, cols), BF16),
            jax.ShapeDtypeStruct((rows, chans, cols), BF16),
            jax.ShapeDtypeStruct((9 * chans, full), F32),
            jax.ShapeDtypeStruct((9 * chans, full), F32),
        ),
        in_specs=[vmem] * 4,
        out_specs=[vmem] * 4,
        scratch_shapes=[
            pltpu.VMEM((4, 4, rows, chans, LANES), BF16),
            pltpu.VMEM((4, 2, 4, chans, LANES), BF16),
            pltpu.VMEM((4, 2, chans, LANES), BF16),
            pltpu.VMEM((wide, lanes), BF16),
            pltpu.VMEM((wide, lanes), BF16),
            pltpu.VMEM((wide, lanes), BF16),
            pltpu.VMEM((3 * chans, wide), BF16),
            pltpu.VMEM((3 * chans, lanes), F32),
            pltpu.VMEM((rows, chans, LANES), F32),
            pltpu.VMEM((2, full, LANES), BF16),
            pltpu.VMEM((3 * chans, lanes), BF16),
            pltpu.VMEM((2, 4, chans, taps), BF16),
            pltpu.VMEM((2, 4, chans, taps), BF16),
            pltpu.VMEM((2, 9 * chans, full), BF16),
            pltpu.VMEM((2, 8, 9 * chans // 4, LANES), BF16),
            pltpu.VMEM((2, 9 * chans, full), BF16),
            dma((4, 3, CHUNKS)),
            dma((4, 3, CHUNKS)),
            dma((4, 2, 4)),
            dma((4, 2, 4)),
            dma((2, 4)),
            dma((2, 4)),
            dma((2, 8)),
            dma((2, 8)),
            dma((2, 8)),
            dma((2, 8)),
        ],
        compiler_params=pltpu.CompilerParams(
            collective_id=0, has_side_effects=True, vmem_limit_bytes=48 * 1024 * 1024
        ),
    )(
        inputs,
        kernel_one.transpose(1, 2, 0, 3).reshape(9, chans, full),
        kernel_two.transpose(1, 2, 0, 3).reshape(9, chans, full),
        cotangent,
    )
    sum_one = sum_one.reshape(3, 3, chans, full).transpose(2, 0, 1, 3)
    sum_two = sum_two.reshape(3, 3, chans, full).transpose(2, 0, 1, 3)
    if not reduce_here:
        sum_one, sum_two = lax.psum((sum_one, sum_two), "space")
    return result, grad_inputs, sum_one, sum_two


def solution(mesh):
    act = P(None, "chan", "space")
    ker = P("chan", None, None, None)
    return jax.shard_map(
        functools.partial(local, mesh.shape["space"]), mesh=mesh,
        in_specs=(act, ker, ker, act), out_specs=(act, act, ker, ker), check_vma=False,
    )
```

```python
import functools

import jax
import jax.numpy as jnp
from jax import lax
from jax.experimental import pallas as pl
from jax.experimental.pallas import tpu as pltpu
from jax.sharding import PartitionSpec as P

F32 = jnp.float32
BF16 = jnp.bfloat16
MESH = pl.DeviceIdType.MESH
LANES = 128
CHUNKS = 4


def kernel(
    n, reduce_here, x_ref, k1_ref, k2_ref, cot_ref, result_ref, gin_ref, g1_ref, g2_ref,
    blocks, halo_in, halo_out, cat_one, cat_two, cat_back, weight, partial, slope_one,
    edges, grad_rows, kt_out, kt_in, sum_out, sum_in, sum_all,
    st_send, st_recv, halo_send, halo_recv, kt_send, kt_recv, rs_send, rs_recv, ag_send, ag_recv,
):
    s, c = lax.axis_index("space"), lax.axis_index("chan")
    rows, chans = x_ref.shape[0], x_ref.shape[1]
    full = 4 * chans
    wide = 3 * full
    high_piece = 9 * chans // 4
    left, right = lax.rem(s + n - 1, n), lax.rem(s + 1, n)
    sibling = c + 1 - 2 * lax.rem(c, 2)
    across = lax.rem(c + 2, 4)
    lane = lax.broadcasted_iota(jnp.int32, (chans, LANES), 1)
    lane_full = lax.broadcasted_iota(jnp.int32, (full, LANES), 1)

    def remote(src, dst, send, recv, to_s, to_c):
        return pltpu.make_async_remote_copy(
            src_ref=src, dst_ref=dst, send_sem=send, recv_sem=recv,
            device_id={"space": to_s, "chan": to_c}, device_id_type=MESH,
        )

    barrier = pltpu.get_barrier_semaphore()
    count = 0
    for d in range(1, 4):
        pl.semaphore_signal(barrier, inc=1, device_id={"space": s, "chan": lax.rem(c + d, 4)}, device_id_type=MESH)
        count += 1
    for side in (left, right):
        for j in range(4):
            pl.semaphore_signal(barrier, inc=1, device_id={"space": side, "chan": j}, device_id_type=MESH)
            count += 1
    if reduce_here:
        for d in range(2, n - 1):
            pl.semaphore_signal(barrier, inc=1, device_id={"space": lax.rem(s + d, n), "chan": c}, device_id_type=MESH)
            count += 1

    def edge_step(p, value, low, high):
        low = jnp.where(lane == p, pltpu.roll(value, p, 1), low)
        high = jnp.where(lane == p, pltpu.roll(value, lax.rem(p + 1, LANES), 1), high)
        return low, high

    zero_edge = jnp.zeros((chans, LANES), F32)
    pending = []

    def send_halo(t, low, high):
        halo_out[t, 0] = low.astype(BF16)
        halo_out[t, 1] = high.astype(BF16)
        for j in range(4):
            for side, to in ((0, left), (1, right)):
                copy = remote(
                    halo_out.at[t, side], halo_in.at[t, 1 - side, c],
                    halo_send.at[t, side, j], halo_recv.at[t, 1 - side, c], to, j,
                )
                copy.start()
                pending.append(copy)

    def send_chunk(t, k, copies):
        step = rows // CHUNKS
        part = pl.ds(k * step, step)
        for held, way, to in zip(copies, (0, 1), (across, sibling)):
            copy = remote(
                blocks.at[t, c, part], blocks.at[t, c, part],
                st_send.at[t, way, k], st_recv.at[t, way, k], s, to,
            )
            copy.start()
            pending.append(copy)
            held.append(copy)

    def collect_stage(t, copies, cat, act, hook=None):
        across_copies, near_copies = copies
        step = rows // CHUNKS
        cat[:, 0:LANES] = jnp.zeros((wide, LANES), BF16)
        cat[:, (rows + 1) * LANES:] = jnp.zeros((wide, LANES), BF16)
        partial[:, 0:LANES] = jnp.zeros((3 * chans, LANES), F32)
        partial[:, (rows + 1) * LANES:] = jnp.zeros((3 * chans, LANES), F32)

        def row_step(p, _):
            value = blocks[t, :, p].reshape(full, LANES)
            at = pl.ds(pl.multiple_of((p + 1) * LANES, LANES), LANES)
            edge_low = pltpu.roll(edges[0], lax.rem(LANES - p, LANES), 1)
            edge_high = pltpu.roll(edges[1], LANES - 1 - p, 1)
            cat[0:full, at] = jnp.where(lane_full == 0, edge_low, pltpu.roll(value, 1, 1))
            cat[full:2 * full, at] = value
            cat[2 * full:, at] = jnp.where(lane_full == LANES - 1, edge_high, pltpu.roll(value, LANES - 1, 1))
            return 0

        def work(k):
            near_copies[k].wait_recv()
            forwards[k].wait_recv()
            lax.fori_loop(k * step, (k + 1) * step, row_step, 0, unroll=True)
            at = slice((k * step + 1) * LANES, ((k + 1) * step + 1) * LANES)
            partial[:, at] = jnp.dot(weight[t], cat[:, at], preferred_element_type=F32)

        def rows_done(k, edge):
            return lax.fori_loop(k * step, (k + 1) * step, act, edge, unroll=True)

        edge, later, forwards = (zero_edge, zero_edge), ([], []), []
        for k in range(CHUNKS):
            across_copies[k].wait_recv()
            part = pl.ds(k * step, step)
            copy = remote(
                blocks.at[t, across, part], blocks.at[t, across, part],
                st_send.at[t, 2, k], st_recv.at[t, 2, k], s, sibling,
            )
            copy.start()
            pending.append(copy)
            forwards.append(copy)
            if k == 0:
                for j in range(4):
                    for side in range(2):
                        remote(
                            halo_out.at[t, side], halo_in.at[t, side, j],
                            halo_send.at[t, side, j], halo_recv.at[t, side, j], left, j,
                        ).wait_recv()
                from_left = halo_in[t, 0].reshape(full, LANES).astype(F32)
                from_right = halo_in[t, 1].reshape(full, LANES).astype(F32)
                edges[0] = jnp.where(s > 0, from_left, 0.0).astype(BF16)
                edges[1] = jnp.where(s < n - 1, from_right, 0.0).astype(BF16)
            else:
                work(k - 1)
            if k >= 2:
                edge = rows_done(k - 2, edge)
                if t < 3:
                    send_chunk(t + 1, k - 2, later)
        gathered = hook() if hook is not None else []
        work(CHUNKS - 1)
        edge = rows_done(CHUNKS - 2, edge)
        edge = rows_done(CHUNKS - 1, edge)
        if t < 3:
            send_halo(t + 1, *edge)
            send_chunk(t + 1, CHUNKS - 2, later)
            send_chunk(t + 1, CHUNKS - 1, later)
        return later, gathered

    def preact(p):
        total = None
        for a in range(3):
            at = pl.ds(pl.multiple_of((p + a) * LANES, LANES), LANES)
            term = partial[a * chans:(a + 1) * chans, at]
            total = term if total is None else total + term
        return total

    def set_weight(t, k_ref):
        for a in range(3):
            for b in range(3):
                weight[t, a * chans:(a + 1) * chans, b * full:(b + 1) * full] = k_ref[3 * a + b]

    def put_grad(p, value):
        for a in range(3):
            at = pl.ds(pl.multiple_of((p + a) * LANES, LANES), LANES)
            grad_rows[a * chans:(a + 1) * chans, at] = value

    def sum_piece(k):
        return (
            pl.ds(pl.multiple_of((k // 2) * high_piece, 16), high_piece),
            pl.ds(pl.multiple_of(lax.rem(k, 2) * LANES, LANES), LANES),
        )

    def kernel_gradient(layer, cat, out_ref):
        total = lax.dot_general(
            grad_rows[...], cat[...], (((1,), (1,)), ((), ())), preferred_element_type=F32
        )
        for a in range(3):
            for b in range(3):
                tap = 3 * a + b
                term = total[a * chans:(a + 1) * chans, b * full:(b + 1) * full]
                if reduce_here:
                    sum_out[layer, tap * chans:(tap + 1) * chans, :] = term.astype(BF16)
                else:
                    out_ref[tap * chans:(tap + 1) * chans, :] = term
        if not reduce_here:
            return []
        copies = []
        for d in range(1, n):
            to = lax.rem(s + d, n)
            rr, ll = sum_piece(to)
            copy = remote(
                sum_out.at[layer, rr, ll], sum_in.at[layer, d],
                rs_send.at[layer, d], rs_recv.at[layer, d], to, c,
            )
            copy.start()
            pending.append(copy)
            copies.append(copy)
        return copies

    def kernel_sum(layer, copies):
        rr, ll = sum_piece(s)
        total = sum_out[layer, rr, ll].astype(F32)
        for d in range(1, n):
            copies[d - 1].wait_recv()
            total = total + sum_in[layer, d].astype(F32)
        sum_all[layer, rr, ll] = total.astype(BF16)
        out = []
        for d in range(1, n):
            to = lax.rem(s + d, n)
            copy = remote(
                sum_all.at[layer, rr, ll], sum_all.at[layer, rr, ll],
                ag_send.at[layer, d], ag_recv.at[layer, d], to, c,
            )
            copy.start()
            pending.append(copy)
            out.append(copy)
        return out

    def send_taps(layer):
        copies = []
        for d in range(1, 4):
            copy = remote(
                kt_out.at[layer, lax.rem(c + d, 4)], kt_in.at[layer, c],
                kt_send.at[layer, d], kt_recv.at[layer, d], s, lax.rem(c + d, 4),
            )
            copy.start()
            pending.append(copy)
            copies.append(copy)
        return copies

    def set_back_weight(layer, copies):
        for copy in copies:
            copy.wait_recv()
        taps = kt_in[layer].reshape(full, kt_in.shape[3]).astype(F32).T.astype(BF16)
        for a in range(3):
            for b in range(3):
                tap = (2 - a) * 3 + 2 - b
                weight[3 - layer, a * chans:(a + 1) * chans, b * full:(b + 1) * full] = taps[tap * chans:(tap + 1) * chans]

    def second(p, edges):
        pre = preact(p)
        sig = jax.nn.sigmoid(pre)
        slope_one[p] = sig * (1.0 + pre * (1.0 - sig))
        value = (pre * sig).astype(BF16)
        blocks[1, c, p] = value
        return edge_step(p, value.astype(F32), *edges)

    def third(p, edges):
        pre = preact(p)
        sig = jax.nn.sigmoid(pre)
        result_ref[p] = (pre * sig).astype(BF16)
        value = (cot_ref[p].astype(F32) * (sig * (1.0 + pre * (1.0 - sig)))).astype(BF16)
        blocks[2, c, p] = value
        put_grad(p, value)
        return edge_step(p, value.astype(F32), *edges)

    def fourth(p, edges):
        value = (preact(p) * slope_one[p]).astype(BF16)
        blocks[3, c, p] = value
        put_grad(p, value)
        return edge_step(p, value.astype(F32), *edges)

    def last(p, edges):
        gin_ref[p] = preact(p).astype(BF16)
        return edges

    def first(p, edges):
        value = x_ref[p]
        blocks[0, c, p] = value
        return edge_step(p, value.astype(F32), *edges)

    low, high = lax.fori_loop(0, rows, first, (zero_edge, zero_edge), unroll=4)
    pl.semaphore_wait(barrier, count)
    send_halo(0, low, high)
    copies = ([], [])
    for k in range(CHUNKS):
        send_chunk(0, k, copies)
    for layer, k_ref in ((0, k1_ref), (1, k2_ref)):
        for j in range(4):
            for tap in range(9):
                kt_out[layer, j, :, tap * chans:(tap + 1) * chans] = (
                    k_ref[tap, :, j * chans:(j + 1) * chans]
                )
            kt_out[layer, j, :, 9 * chans:] = jnp.zeros((chans, kt_out.shape[3] - 9 * chans), BF16)
        kt_in[layer, c] = kt_out[layer, c]
    back_two = send_taps(1)
    set_weight(0, k1_ref)
    set_weight(1, k2_ref)
    grad_rows[...] = jnp.zeros(grad_rows.shape, BF16)
    copies, _ = collect_stage(0, copies, cat_one, second)


    back_one = send_taps(0)
    set_back_weight(1, back_two)
    copies, _ = collect_stage(1, copies, cat_two, third)


    reduce_two = kernel_gradient(1, cat_two, g2_ref)
    set_back_weight(0, back_one)
    copies, gather_two = collect_stage(
        2, copies, cat_back, fourth, functools.partial(kernel_sum, 1, reduce_two) if reduce_here else None
    )


    reduce_one = kernel_gradient(0, cat_one, g1_ref)
    _, gather_one = collect_stage(
        3, copies, cat_back, last, functools.partial(kernel_sum, 0, reduce_one) if reduce_here else None
    )


    if reduce_here:
        for layer, out, ref in ((1, gather_two, g2_ref), (0, gather_one, g1_ref)):
            for copy in out:
                copy.wait_recv()
            ref[...] = sum_all[layer]
    for copy in pending:
        copy.wait_send()


def local(n, inputs, kernel_one, kernel_two, cotangent):
    rows, chans, cols = inputs.shape
    full = 4 * chans
    wide = 3 * full
    reduce_here = n == 8
    lanes = (rows + 2) * LANES
    taps = -(-9 * chans // LANES) * LANES
    dma = pltpu.SemaphoreType.DMA
    vmem = pl.BlockSpec(memory_space=pltpu.VMEM)
    result, grad_inputs, sum_one, sum_two = pl.pallas_call(
        functools.partial(kernel, n, reduce_here),
        out_shape=(
            jax.ShapeDtypeStruct((rows, chans, cols), BF16),
            jax.ShapeDtypeStruct((rows, chans, cols), BF16),
            jax.ShapeDtypeStruct((9 * chans, full), BF16 if reduce_here else F32),
            jax.ShapeDtypeStruct((9 * chans, full), BF16 if reduce_here else F32),
        ),
        in_specs=[vmem] * 4,
        out_specs=[vmem] * 4,
        scratch_shapes=[
            pltpu.VMEM((4, 4, rows, chans, LANES), BF16),
            pltpu.VMEM((4, 2, 4, chans, LANES), BF16),
            pltpu.VMEM((4, 2, chans, LANES), BF16),
            pltpu.VMEM((wide, lanes), BF16),
            pltpu.VMEM((wide, lanes), BF16),
            pltpu.VMEM((wide, lanes), BF16),
            pltpu.VMEM((4, 3 * chans, wide), BF16),
            pltpu.VMEM((3 * chans, lanes), F32),
            pltpu.VMEM((rows, chans, LANES), F32),
            pltpu.VMEM((2, full, LANES), BF16),
            pltpu.VMEM((3 * chans, lanes), BF16),
            pltpu.VMEM((2, 4, chans, taps), BF16),
            pltpu.VMEM((2, 4, chans, taps), BF16),
            pltpu.VMEM((2, 9 * chans, full), BF16),
            pltpu.VMEM((2, 8, 9 * chans // 4, LANES), BF16),
            pltpu.VMEM((2, 9 * chans, full), BF16),
            dma((4, 3, CHUNKS)),
            dma((4, 3, CHUNKS)),
            dma((4, 2, 4)),
            dma((4, 2, 4)),
            dma((2, 4)),
            dma((2, 4)),
            dma((2, 8)),
            dma((2, 8)),
            dma((2, 8)),
            dma((2, 8)),
        ],
        compiler_params=pltpu.CompilerParams(
            collective_id=0, has_side_effects=True, vmem_limit_bytes=48 * 1024 * 1024
        ),
    )(
        inputs,
        kernel_one.transpose(1, 2, 0, 3).reshape(9, chans, full),
        kernel_two.transpose(1, 2, 0, 3).reshape(9, chans, full),
        cotangent,
    )
    sum_one = sum_one.astype(F32).reshape(3, 3, chans, full).transpose(2, 0, 1, 3)
    sum_two = sum_two.astype(F32).reshape(3, 3, chans, full).transpose(2, 0, 1, 3)
    if not reduce_here:
        sum_one, sum_two = lax.psum((sum_one, sum_two), "space")
    return result, grad_inputs, sum_one, sum_two


def solution(mesh):
    act = P(None, "chan", "space")
    ker = P("chan", None, None, None)
    return jax.shard_map(
        functools.partial(local, mesh.shape["space"]), mesh=mesh,
        in_specs=(act, ker, ker, act), out_specs=(act, act, ker, ker), check_vma=False,
    )
```

```python
import functools

import jax
import jax.numpy as jnp
from jax import lax
from jax.experimental import pallas as pl
from jax.experimental.pallas import tpu as pltpu
from jax.sharding import PartitionSpec as P

F32 = jnp.float32
BF16 = jnp.bfloat16
MESH = pl.DeviceIdType.MESH
LANES = 128
CHUNKS = 4


def kernel(
    n, reduce_here, x_ref, k1_ref, k2_ref, cot_ref, result_ref, gin_ref, g1_ref, g2_ref,
    blocks, halo_in, halo_out, cat_one, cat_two, cat_back, weight, partial, slope_one,
    edges, grad_rows, kt_out, kt_in, sum_out, sum_in, sum_all,
    st_send, st_recv, halo_send, halo_recv, kt_send, kt_recv, rs_send, rs_recv, ag_send, ag_recv,
):
    s, c = lax.axis_index("space"), lax.axis_index("chan")
    rows, chans = x_ref.shape[0], x_ref.shape[1]
    full = 4 * chans
    wide = 3 * full
    high_piece = 9 * chans // 4
    left, right = lax.rem(s + n - 1, n), lax.rem(s + 1, n)
    sibling = c + 1 - 2 * lax.rem(c, 2)
    across = lax.rem(c + 2, 4)
    lane = lax.broadcasted_iota(jnp.int32, (chans, LANES), 1)
    lane_full = lax.broadcasted_iota(jnp.int32, (full, LANES), 1)

    def remote(src, dst, send, recv, to_s, to_c):
        return pltpu.make_async_remote_copy(
            src_ref=src, dst_ref=dst, send_sem=send, recv_sem=recv,
            device_id={"space": to_s, "chan": to_c}, device_id_type=MESH,
        )

    barrier = pltpu.get_barrier_semaphore()
    count = 0
    for d in range(1, 4):
        pl.semaphore_signal(barrier, inc=1, device_id={"space": s, "chan": lax.rem(c + d, 4)}, device_id_type=MESH)
        count += 1
    for side in (left, right):
        for j in range(4):
            pl.semaphore_signal(barrier, inc=1, device_id={"space": side, "chan": j}, device_id_type=MESH)
            count += 1
    if reduce_here:
        for d in range(2, n - 1):
            pl.semaphore_signal(barrier, inc=1, device_id={"space": lax.rem(s + d, n), "chan": c}, device_id_type=MESH)
            count += 1

    def edge_step(p, value, low, high):
        low = jnp.where(lane == p, pltpu.roll(value, p, 1), low)
        high = jnp.where(lane == p, pltpu.roll(value, lax.rem(p + 1, LANES), 1), high)
        return low, high

    zero_edge = jnp.zeros((chans, LANES), F32)
    pending = []

    def send_halo(t, low, high):
        halo_out[t, 0] = low.astype(BF16)
        halo_out[t, 1] = high.astype(BF16)
        for j in range(4):
            for side, to in ((0, left), (1, right)):
                copy = remote(
                    halo_out.at[t, side], halo_in.at[t, 1 - side, c],
                    halo_send.at[t, side, j], halo_recv.at[t, 1 - side, c], to, j,
                )
                copy.start()
                pending.append(copy)

    def send_chunk(t, k, copies):
        step = rows // CHUNKS
        part = pl.ds(k * step, step)
        for held, way, to in zip(copies, (0, 1), (across, sibling)):
            copy = remote(
                blocks.at[t, c, part], blocks.at[t, c, part],
                st_send.at[t, way, k], st_recv.at[t, way, k], s, to,
            )
            copy.start()
            pending.append(copy)
            held.append(copy)

    def collect_stage(t, copies, cat, act, hook=None):
        across_copies, near_copies = copies
        step = rows // CHUNKS
        cat[:, 0:LANES] = jnp.zeros((wide, LANES), BF16)
        cat[:, (rows + 1) * LANES:] = jnp.zeros((wide, LANES), BF16)
        partial[:, 0:LANES] = jnp.zeros((3 * chans, LANES), F32)
        partial[:, (rows + 1) * LANES:] = jnp.zeros((3 * chans, LANES), F32)

        def row_step(p, _):
            value = blocks[t, :, p].reshape(full, LANES)
            at = pl.ds(pl.multiple_of((p + 1) * LANES, LANES), LANES)
            edge_low = pltpu.roll(edges[0], lax.rem(LANES - p, LANES), 1)
            edge_high = pltpu.roll(edges[1], LANES - 1 - p, 1)
            cat[0:full, at] = jnp.where(lane_full == 0, edge_low, pltpu.roll(value, 1, 1))
            cat[full:2 * full, at] = value
            cat[2 * full:, at] = jnp.where(lane_full == LANES - 1, edge_high, pltpu.roll(value, LANES - 1, 1))
            return 0

        def work(k):
            near_copies[k].wait_recv()
            forwards[k].wait_recv()
            lax.fori_loop(k * step, (k + 1) * step, row_step, 0, unroll=True)
            at = slice((k * step + 1) * LANES, ((k + 1) * step + 1) * LANES)
            partial[:, at] = jnp.dot(weight[t], cat[:, at], preferred_element_type=F32)

        def rows_done(k, edge):
            return lax.fori_loop(k * step, (k + 1) * step, act, edge, unroll=True)

        edge, later, forwards = (zero_edge, zero_edge), ([], []), []
        for k in range(CHUNKS):
            across_copies[k].wait_recv()
            part = pl.ds(k * step, step)
            copy = remote(
                blocks.at[t, across, part], blocks.at[t, across, part],
                st_send.at[t, 2, k], st_recv.at[t, 2, k], s, sibling,
            )
            copy.start()
            pending.append(copy)
            forwards.append(copy)
            if k == 0:
                for j in range(4):
                    for side in range(2):
                        remote(
                            halo_out.at[t, side], halo_in.at[t, side, j],
                            halo_send.at[t, side, j], halo_recv.at[t, side, j], left, j,
                        ).wait_recv()
                from_left = halo_in[t, 0].reshape(full, LANES).astype(F32)
                from_right = halo_in[t, 1].reshape(full, LANES).astype(F32)
                edges[0] = jnp.where(s > 0, from_left, 0.0).astype(BF16)
                edges[1] = jnp.where(s < n - 1, from_right, 0.0).astype(BF16)
            else:
                work(k - 1)
            if k >= 2:
                edge = rows_done(k - 2, edge)
                if t < 3:
                    send_chunk(t + 1, k - 2, later)
        gathered = hook() if hook is not None else []
        work(CHUNKS - 1)
        edge = rows_done(CHUNKS - 2, edge)
        if t < 3:
            send_chunk(t + 1, CHUNKS - 2, later)
        edge = rows_done(CHUNKS - 1, edge)
        if t < 3:
            send_halo(t + 1, *edge)
            send_chunk(t + 1, CHUNKS - 1, later)
        return later, gathered

    def preact(p):
        total = None
        for a in range(3):
            at = pl.ds(pl.multiple_of((p + a) * LANES, LANES), LANES)
            term = partial[a * chans:(a + 1) * chans, at]
            total = term if total is None else total + term
        return total

    def set_weight(t, k_ref):
        for a in range(3):
            for b in range(3):
                weight[t, a * chans:(a + 1) * chans, b * full:(b + 1) * full] = k_ref[3 * a + b]

    def put_grad(p, value):
        for a in range(3):
            at = pl.ds(pl.multiple_of((p + a) * LANES, LANES), LANES)
            grad_rows[a * chans:(a + 1) * chans, at] = value

    def sum_piece(k):
        return (
            pl.ds(pl.multiple_of((k // 2) * high_piece, 16), high_piece),
            pl.ds(pl.multiple_of(lax.rem(k, 2) * LANES, LANES), LANES),
        )

    def kernel_gradient(layer, cat, out_ref):
        total = lax.dot_general(
            grad_rows[...], cat[...], (((1,), (1,)), ((), ())), preferred_element_type=F32
        )
        for a in range(3):
            for b in range(3):
                tap = 3 * a + b
                term = total[a * chans:(a + 1) * chans, b * full:(b + 1) * full]
                if reduce_here:
                    sum_out[layer, tap * chans:(tap + 1) * chans, :] = term.astype(BF16)
                else:
                    out_ref[tap * chans:(tap + 1) * chans, :] = term
        if not reduce_here:
            return []
        copies = []
        for d in range(1, n):
            to = lax.rem(s + d, n)
            rr, ll = sum_piece(to)
            copy = remote(
                sum_out.at[layer, rr, ll], sum_in.at[layer, d],
                rs_send.at[layer, d], rs_recv.at[layer, d], to, c,
            )
            copy.start()
            pending.append(copy)
            copies.append(copy)
        return copies

    def kernel_sum(layer, copies):
        rr, ll = sum_piece(s)
        total = sum_out[layer, rr, ll].astype(F32)
        for d in range(1, n):
            copies[d - 1].wait_recv()
            total = total + sum_in[layer, d].astype(F32)
        sum_all[layer, rr, ll] = total.astype(BF16)
        out = []
        for d in range(1, n):
            to = lax.rem(s + d, n)
            copy = remote(
                sum_all.at[layer, rr, ll], sum_all.at[layer, rr, ll],
                ag_send.at[layer, d], ag_recv.at[layer, d], to, c,
            )
            copy.start()
            pending.append(copy)
            out.append(copy)
        return out

    def send_taps(layer):
        copies = []
        for d in range(1, 4):
            copy = remote(
                kt_out.at[layer, lax.rem(c + d, 4)], kt_in.at[layer, c],
                kt_send.at[layer, d], kt_recv.at[layer, d], s, lax.rem(c + d, 4),
            )
            copy.start()
            pending.append(copy)
            copies.append(copy)
        return copies

    def set_back_weight(layer, copies):
        for copy in copies:
            copy.wait_recv()
        taps = kt_in[layer].reshape(full, kt_in.shape[3]).astype(F32).T.astype(BF16)
        for a in range(3):
            for b in range(3):
                tap = (2 - a) * 3 + 2 - b
                weight[3 - layer, a * chans:(a + 1) * chans, b * full:(b + 1) * full] = taps[tap * chans:(tap + 1) * chans]

    def second(p, edges):
        pre = preact(p)
        sig = jax.nn.sigmoid(pre)
        slope_one[p] = sig * (1.0 + pre * (1.0 - sig))
        value = (pre * sig).astype(BF16)
        blocks[1, c, p] = value
        return edge_step(p, value.astype(F32), *edges)

    def third(p, edges):
        pre = preact(p)
        sig = jax.nn.sigmoid(pre)
        result_ref[p] = (pre * sig).astype(BF16)
        value = (cot_ref[p].astype(F32) * (sig * (1.0 + pre * (1.0 - sig)))).astype(BF16)
        blocks[2, c, p] = value
        put_grad(p, value)
        return edge_step(p, value.astype(F32), *edges)

    def fourth(p, edges):
        value = (preact(p) * slope_one[p]).astype(BF16)
        blocks[3, c, p] = value
        put_grad(p, value)
        return edge_step(p, value.astype(F32), *edges)

    def last(p, edges):
        gin_ref[p] = preact(p).astype(BF16)
        return edges

    def first(p, edges):
        value = x_ref[p]
        blocks[0, c, p] = value
        return edge_step(p, value.astype(F32), *edges)

    low, high = lax.fori_loop(0, rows, first, (zero_edge, zero_edge), unroll=4)
    pl.semaphore_wait(barrier, count)
    send_halo(0, low, high)
    copies = ([], [])
    for k in range(CHUNKS):
        send_chunk(0, k, copies)
    for layer, k_ref in ((0, k1_ref), (1, k2_ref)):
        for j in range(4):
            for tap in range(9):
                kt_out[layer, j, :, tap * chans:(tap + 1) * chans] = (
                    k_ref[tap, :, j * chans:(j + 1) * chans]
                )
            kt_out[layer, j, :, 9 * chans:] = jnp.zeros((chans, kt_out.shape[3] - 9 * chans), BF16)
        kt_in[layer, c] = kt_out[layer, c]
    back_two = send_taps(1)
    set_weight(0, k1_ref)
    set_weight(1, k2_ref)
    grad_rows[...] = jnp.zeros(grad_rows.shape, BF16)
    copies, _ = collect_stage(0, copies, cat_one, second)


    back_one = send_taps(0)
    set_back_weight(1, back_two)
    copies, _ = collect_stage(1, copies, cat_two, third)


    reduce_two = kernel_gradient(1, cat_two, g2_ref)
    set_back_weight(0, back_one)
    copies, gather_two = collect_stage(
        2, copies, cat_back, fourth, functools.partial(kernel_sum, 1, reduce_two) if reduce_here else None
    )


    reduce_one = kernel_gradient(0, cat_one, g1_ref)
    _, gather_one = collect_stage(
        3, copies, cat_back, last, functools.partial(kernel_sum, 0, reduce_one) if reduce_here else None
    )


    if reduce_here:
        for layer, out, ref in ((1, gather_two, g2_ref), (0, gather_one, g1_ref)):
            for copy in out:
                copy.wait_recv()
            ref[...] = sum_all[layer]
    for copy in pending:
        copy.wait_send()


def local(n, inputs, kernel_one, kernel_two, cotangent):
    rows, chans, cols = inputs.shape
    full = 4 * chans
    wide = 3 * full
    reduce_here = n == 8
    lanes = (rows + 2) * LANES
    taps = -(-9 * chans // LANES) * LANES
    dma = pltpu.SemaphoreType.DMA
    vmem = pl.BlockSpec(memory_space=pltpu.VMEM)
    result, grad_inputs, sum_one, sum_two = pl.pallas_call(
        functools.partial(kernel, n, reduce_here),
        out_shape=(
            jax.ShapeDtypeStruct((rows, chans, cols), BF16),
            jax.ShapeDtypeStruct((rows, chans, cols), BF16),
            jax.ShapeDtypeStruct((9 * chans, full), BF16 if reduce_here else F32),
            jax.ShapeDtypeStruct((9 * chans, full), BF16 if reduce_here else F32),
        ),
        in_specs=[vmem] * 4,
        out_specs=[vmem] * 4,
        scratch_shapes=[
            pltpu.VMEM((4, 4, rows, chans, LANES), BF16),
            pltpu.VMEM((4, 2, 4, chans, LANES), BF16),
            pltpu.VMEM((4, 2, chans, LANES), BF16),
            pltpu.VMEM((wide, lanes), BF16),
            pltpu.VMEM((wide, lanes), BF16),
            pltpu.VMEM((wide, lanes), BF16),
            pltpu.VMEM((4, 3 * chans, wide), BF16),
            pltpu.VMEM((3 * chans, lanes), F32),
            pltpu.VMEM((rows, chans, LANES), F32),
            pltpu.VMEM((2, full, LANES), BF16),
            pltpu.VMEM((3 * chans, lanes), BF16),
            pltpu.VMEM((2, 4, chans, taps), BF16),
            pltpu.VMEM((2, 4, chans, taps), BF16),
            pltpu.VMEM((2, 9 * chans, full), BF16),
            pltpu.VMEM((2, 8, 9 * chans // 4, LANES), BF16),
            pltpu.VMEM((2, 9 * chans, full), BF16),
            dma((4, 3, CHUNKS)),
            dma((4, 3, CHUNKS)),
            dma((4, 2, 4)),
            dma((4, 2, 4)),
            dma((2, 4)),
            dma((2, 4)),
            dma((2, 8)),
            dma((2, 8)),
            dma((2, 8)),
            dma((2, 8)),
        ],
        compiler_params=pltpu.CompilerParams(
            collective_id=0, has_side_effects=True, vmem_limit_bytes=48 * 1024 * 1024
        ),
    )(
        inputs,
        kernel_one.transpose(1, 2, 0, 3).reshape(9, chans, full),
        kernel_two.transpose(1, 2, 0, 3).reshape(9, chans, full),
        cotangent,
    )
    sum_one = sum_one.astype(F32).reshape(3, 3, chans, full).transpose(2, 0, 1, 3)
    sum_two = sum_two.astype(F32).reshape(3, 3, chans, full).transpose(2, 0, 1, 3)
    if not reduce_here:
        sum_one, sum_two = lax.psum((sum_one, sum_two), "space")
    return result, grad_inputs, sum_one, sum_two


def solution(mesh):
    act = P(None, "chan", "space")
    ker = P("chan", None, None, None)
    return jax.shard_map(
        functools.partial(local, mesh.shape["space"]), mesh=mesh,
        in_specs=(act, ker, ker, act), out_specs=(act, act, ker, ker), check_vma=False,
    )
```
